1024 devices in a mesh: section: 16 (over y_lo, x, core), expert: 64 (over y_hi, z).
Axes of the slice: x: 4, y: 4 (y_hi: 2, y_lo: 2; y = y_hi * 2 + y_lo), z: 32, core: 2. Of those that a mesh axis runs over, the one named last changes fastest.
Arguments:
- held_up: bfloat16 [16, 128, 28672], P('section', None, 'expert'), may hold values from -6 to 6
- held_down: bfloat16 [16, 128, 28672], P('section', None, 'expert'), may hold values from -6 to 6
- routes_up: int32 [16, 512, 8], P('section'), may hold values from 0 to 255, as said below
- routes_down: int32 [16, 512, 8], P('section'), may hold values from 0 to 255, as said below
- gates_up: float32 [16, 512, 8], P('section'), may hold values from 0.5 to 2.5
- gates_down: float32 [16, 512, 8], P('section'), may hold values from 0.5 to 2.5
- capacity: int32 [16, 4], P('section'), may hold values from 40 to 80, as said below
- w_gate: bfloat16 [16, 28672, 1024], P('section', 'expert'), may hold values from -0.0625 to 0.0625
- w_up: bfloat16 [16, 28672, 1024], P('section', 'expert'), may hold values from -0.0625 to 0.0625
- w_down: bfloat16 [16, 28672, 1024], P('section', 'expert'), may hold values from -0.1875 to 0.1875
Outputs:
- arrived_up: bfloat16 [16, 128, 28672], P('section', None, 'expert')
- arrived_down: bfloat16 [16, 128, 28672], P('section', None, 'expert')
The draws below stay inside these ranges and needn't reach their ends.
Inputs may be any that keep to these rules, and one draw needn't show every extreme that they name: `routes_up`: each row names 8 different experts. At some section an expert in flight has capacity 80 and is named by at least 80 upward rows of every group. `routes_down`: each row names 8 different experts. At some section one expert in flight has capacity 80.
All inputs are finite; a program needn't handle non-finite values.
Results may differ from the reference program's by a relative error of at most 0.0051.
Values may be sent and summed in bfloat16 or wider, within the bound.
No kernel may reach another device: no remote copies, remote signals or barrier semaphores. Data moves between devices by JAX's collectives and lax.ppermute only.
A program may use at most 32 MiB of HBM per device.

```python
import jax
import jax.numpy as jnp
from jax import lax

D = 7168
EXPERTS = 256
TOPK = 8
H = 1024
TOK_G = 128
LAYERS = 16
NG = 4
CAP = 80


def hot_pick(key):
    first_key, second_key, third_key = jax.random.split(jax.random.fold_in(key, 77), 3)
    hot_expert = jax.random.randint(first_key, (LAYERS,), 0, NG)
    offset = jax.random.randint(second_key, (LAYERS,), 0, TOK_G)
    hot_section = jax.random.randint(third_key, (), 0, LAYERS)
    return (hot_expert, offset, hot_section)


def route_table(key, hot_expert, offset, forced):
    row_count = NG * TOK_G
    key_hit, key_noise, key_order = jax.random.split(key, 3)
    hit_mask = jax.random.randint(key_hit, (LAYERS, row_count, NG), 0, 4) == 0
    if forced:
        positions = jnp.arange(row_count, dtype=jnp.int32) % TOK_G
        force_rows = (positions[None, :] + offset[:, None]) % TOK_G < CAP
        force_expert = jnp.arange(NG, dtype=jnp.int32)[None, None, :] == hot_expert[:, None, None]
        hit_mask = hit_mask | force_rows[:, :, None] & force_expert
    padding = jnp.zeros((LAYERS, row_count, EXPERTS - NG), dtype=bool)
    hit_full = jnp.concatenate([hit_mask, padding], axis=2)
    expert_ids = jnp.arange(EXPERTS, dtype=jnp.int32)
    in_window = expert_ids < NG
    noise = jax.random.randint(key_noise, (LAYERS, row_count, EXPERTS), 1, 1 << 20)
    scores = jnp.where(in_window, jnp.where(hit_full, (1 << 28) + expert_ids, -1 - expert_ids), noise * 256 + expert_ids)
    _, chosen = lax.top_k(scores, TOPK)
    shuffle = jax.random.randint(key_order, (LAYERS, row_count, TOPK), 0, 1 << 20) * TOPK + jnp.arange(TOPK, dtype=jnp.int32)
    order = jnp.argsort(shuffle, axis=-1, stable=True)
    return jnp.take_along_axis(chosen, order, axis=-1).astype(jnp.int32)


def draw_routes_up(key, part):
    hot_expert, offset, hot_section = hot_pick(key)
    key = jax.random.fold_in(key, 1)
    return route_table(key, hot_expert, offset, True)


def draw_routes_down(key, part):
    key = jax.random.fold_in(key, 2)
    return route_table(key, None, None, False)


def draw_capacity(key, part):
    hot_expert, offset, hot_section = hot_pick(key)
    key = jax.random.fold_in(key, 3)
    values = jax.random.randint(key, (LAYERS, NG), CAP // 2, CAP + 1)
    expert_ids = jnp.arange(NG, dtype=jnp.int32)[None, :]
    section_ids = jnp.arange(LAYERS, dtype=jnp.int32)[:, None]
    is_hot = (expert_ids == hot_expert[:, None]) & (section_ids == hot_section)
    if NG > 1:
        is_low = expert_ids == (hot_expert[:, None] + 1) % NG
        values = jnp.where(is_low, CAP // 2, values)
    return jnp.where(is_hot, CAP, values).astype(jnp.int32)


def block_levels(rng, dims, cuts, low, high):
    def one(axis_at, blocks):
        steps = jax.random.uniform(jax.random.fold_in(jax.random.fold_in(rng, 6), axis_at), (blocks,), jnp.float32, low / len(cuts), high / len(cuts))
        return jnp.repeat(jnp.exp(steps), dims[axis_at] // blocks).reshape((-1,) + (1,) * (len(dims) - axis_at - 1))

    level = one(*cuts[0])
    for cut in cuts[1:]:
        level = level * one(*cut)
    return level


def bell_draw(stream_key, extent, width, most, pieces=(), held_as=jnp.bfloat16):
    drawn = width * jax.random.normal(stream_key, extent, jnp.float32)
    if pieces:
        drawn = drawn * block_levels(stream_key, extent, pieces, -0.22, 0.18)
    return jnp.clip(drawn, -most, most).astype(held_as)


def setup_inputs(seed: int = 0) -> dict:
    splits = jax.random.split(jax.random.key(seed), 11)
    return {
        "held_up": bell_draw(splits[0], (LAYERS, TOK_G, NG * D), 1.0, 6.0, ((0, 16), (2, 64))),
        "held_down": bell_draw(splits[1], (LAYERS, TOK_G, NG * D), 1.0, 6.0, ((0, 16), (2, 64))),
        "routes_up": draw_routes_up(jax.random.fold_in(splits[10], 71), 0),
        "routes_down": draw_routes_down(jax.random.fold_in(splits[10], 71), 0),
        "gates_up": jnp.clip(0.5 + 2.0 * jax.random.uniform(splits[4], (LAYERS, NG * TOK_G, TOPK), jnp.float32) ** block_levels(splits[4], (LAYERS, NG * TOK_G, TOPK), ((0, 16),), -0.2, 0.2), 0.5, 2.5),
        "gates_down": jnp.clip(0.5 + 2.0 * jax.random.uniform(splits[5], (LAYERS, NG * TOK_G, TOPK), jnp.float32) ** block_levels(splits[5], (LAYERS, NG * TOK_G, TOPK), ((0, 16),), -0.2, 0.2), 0.5, 2.5),
        "capacity": draw_capacity(jax.random.fold_in(splits[10], 71), 0),
        "w_gate": bell_draw(splits[7], (LAYERS, NG * D, H), D ** -0.5, 0.0625, ((0, 16), (1, 64))),
        "w_up": bell_draw(splits[8], (LAYERS, NG * D, H), D ** -0.5, 0.0625, ((0, 16), (1, 64))),
        "w_down": bell_draw(splits[9], (LAYERS, NG * D, H), H ** -0.5, 0.1875, ((0, 16), (1, 64))),
    }


def one_section(section_args):
    up_rows, down_rows, route_up, route_down, gate_up, gate_down, cap_row, gate_mat, up_mat, down_mat = section_args
    up_block = up_rows.reshape(TOK_G, NG, D).transpose(1, 0, 2)
    down_block = down_rows.reshape(TOK_G, NG, D).transpose(1, 0, 2)
    block = jnp.concatenate([up_block, down_block], axis=1)
    routes = jnp.concatenate([route_up.reshape(NG, TOK_G, TOPK), route_down.reshape(NG, TOK_G, TOPK)], axis=1)
    gates = jnp.concatenate([gate_up.reshape(NG, TOK_G, TOPK), gate_down.reshape(NG, TOK_G, TOPK)], axis=1)
    window_ids = jnp.arange(NG, dtype=jnp.int32)
    matches = routes[:, :, :, None] == window_ids[None, None, None, :]
    hit_mask = jnp.sum(matches.astype(jnp.int32), axis=2)
    gate_sel = jnp.sum(jnp.where(matches, gates[:, :, :, None], jnp.float32(0.0)), axis=2)
    rank_before = jnp.cumsum(hit_mask, axis=1) - hit_mask
    kept_mask = hit_mask * (rank_before < cap_row[None, None, :]).astype(jnp.int32)
    slot_ids = jnp.arange(CAP, dtype=jnp.int32)
    slot_mask = (kept_mask[:, :, :, None] == 1) & (rank_before[:, :, :, None] == slot_ids[None, None, None, :])
    slot_float = slot_mask.astype(jnp.float32)
    slot_rows = jnp.einsum("grec,grd->egcd", slot_float, block.astype(jnp.float32),
                           precision=lax.Precision.HIGHEST).astype(jnp.bfloat16)

    def one_expert(expert_args):
        rows_in, gate_w, up_w, down_w = expert_args
        gate_pre = jnp.dot(rows_in, gate_w, preferred_element_type=jnp.float32)
        up_pre = jnp.dot(rows_in, up_w, preferred_element_type=jnp.float32)
        hidden = (jax.nn.silu(gate_pre) * up_pre).astype(jnp.bfloat16)
        return lax.dot_general(hidden, down_w, (((1,), (1,)), ((), ())),
                               preferred_element_type=jnp.float32).astype(jnp.bfloat16)

    expert_out = lax.map(one_expert, (slot_rows.reshape(NG, NG * CAP, D), gate_mat.reshape(NG, D, H),
                                      up_mat.reshape(NG, D, H), down_mat.reshape(NG, D, H)))
    expert_out = expert_out.reshape(NG, NG, CAP, D)
    combine_weights = slot_float * gate_sel[:, :, :, None]
    branch_sum = jnp.einsum("grec,egcd->grd", combine_weights, expert_out.astype(jnp.float32),
                            precision=lax.Precision.HIGHEST)
    finished = (block.astype(jnp.float32) + branch_sum).astype(jnp.bfloat16)
    out_up = finished[:, :TOK_G].transpose(1, 0, 2).reshape(TOK_G, NG * D)
    out_down = finished[:, TOK_G:].transpose(1, 0, 2).reshape(TOK_G, NG * D)
    return out_up, out_down


def reference(held_up, held_down, routes_up, routes_down, gates_up, gates_down, capacity, w_gate, w_up, w_down):
    out_up, out_down = lax.map(one_section, (held_up, held_down, routes_up, routes_down, gates_up, gates_down,
                                           capacity, w_gate, w_up, w_down))
    arrived_up = jnp.roll(out_up, 1, axis=0)
    arrived_down = jnp.roll(out_down, -1, axis=0)
    return arrived_up, arrived_down
```

```python
import functools

import jax
import jax.numpy as jnp
from jax import lax
from jax.experimental import pallas as pl
from jax.experimental.pallas import tpu as pltpu
from jax.sharding import PartitionSpec as P

SUM = jnp.float16
PARTS = 16
GROUPS = 4
DEEP = 18
VMEM = pltpu.VMEM
SMEM = pltpu.SMEM
VMEM_LIMIT = 40 * 1024 * 1024


def swap(value, pattern):
    count = lax.axis_size("expert")
    return lax.ppermute(value, "expert", [(i, i ^ pattern) for i in range(count)])


def along(value, pairs):
    groups = lax.axis_size("expert") // PARTS
    return lax.ppermute(value, "expert", [(g * PARTS + a, g * PARTS + b) for g in range(groups) for a, b in pairs])


def shift(value, axis, steps):
    count = lax.axis_size(axis)
    return lax.ppermute(value, axis, [(i, (i + steps) % count) for i in range(count)])


def call(kernel, out_shape, in_spaces, args, scratch=(), after=(), flops=0, moved=0):
    taken = len(args)

    def body(*refs):
        kernel(*refs[:taken], *refs[taken + len(after) :])

    return pl.pallas_call(
        body,
        out_shape=out_shape,
        in_specs=[pl.BlockSpec(memory_space=space) for space in in_spaces + [pl.ANY] * len(after)],
        out_specs=jax.tree.map(lambda _: pl.BlockSpec(memory_space=VMEM), out_shape),
        scratch_shapes=list(scratch),
        compiler_params=pltpu.CompilerParams(vmem_limit_bytes=VMEM_LIMIT),
        cost_estimate=pl.CostEstimate(flops=flops, bytes_accessed=moved, transcendentals=0),
    )(*args, *after)


def route_kernel(cap, place_ref, up_ref, down_ref, ru_ref, rd_ref, gu_ref, gd_ref, capacity_ref,
                 own_ref, sent_ref, across_ref, mask_ref, share_ref):
    slot_refs = {0: own_ref, 1: across_ref.at[0], 2: sent_ref.at[0], 3: sent_ref.at[1]}
    group = place_ref[0]
    tokens = up_ref.shape[1]
    rows = 2 * tokens
    start = pl.multiple_of(group * tokens, tokens)
    routes = jnp.concatenate([ru_ref[:, pl.ds(start, tokens)], rd_ref[:, pl.ds(start, tokens)]], axis=1)
    gates = jnp.concatenate([gu_ref[:, pl.ds(start, tokens)], gd_ref[:, pl.ds(start, tokens)]], axis=1)
    hits, shares = [], []
    for k in range(GROUPS):
        match = routes == (group ^ k)
        hits.append(jnp.sum(jnp.where(match, 1.0, 0.0), axis=0, keepdims=True))
        shares.append(jnp.sum(jnp.where(match, gates, 0.0), axis=0, keepdims=True))
    pad = [jnp.zeros((8 - GROUPS, rows), jnp.float32)]
    hit = jnp.concatenate(hits + pad, axis=0)
    share_ref[...] = jnp.concatenate(shares + pad, axis=0)
    before = lax.broadcasted_iota(jnp.int32, (rows, rows), 0) < lax.broadcasted_iota(jnp.int32, (rows, rows), 1)
    rank = jnp.dot(hit.astype(jnp.bfloat16), jnp.where(before, 1.0, 0.0).astype(jnp.bfloat16),
                   preferred_element_type=jnp.float32)
    block = jnp.concatenate([up_ref[...], down_ref[...]], axis=1)
    slot_ids = lax.broadcasted_iota(jnp.int32, (cap, rows), 0)
    for k in (2, 3, 1, 0):
        limit = capacity_ref[0, group ^ k].astype(jnp.float32)
        kept = (hit[k : k + 1] > 0.5) & (rank[k : k + 1] < limit)
        target = jnp.where(kept, rank[k : k + 1], -1.0).astype(jnp.int32)
        mask = jnp.where(target == slot_ids, 1.0, 0.0).astype(jnp.bfloat16)
        mask_ref[k] = mask
        slot_refs[k][...] = lax.dot_general(
            mask, block, (((1,), (1,)), ((), ())), preferred_element_type=jnp.float32
        ).astype(jnp.bfloat16)


def up_kernel(place_ref, first_ref, second_ref, gate_ref, up_ref, keep_ref, right_ref, left_ref, blocks):
    part = place_ref[1]
    half = first_ref.shape[0]
    x = jnp.concatenate([first_ref[...], second_ref[...]], axis=0)
    for n in range(8):
        column = slice(n * 128, n * 128 + 128)
        for z, ref in enumerate((gate_ref, up_ref)):
            result = jnp.dot(x, ref[:, column], preferred_element_type=jnp.float32)
            blocks[n, :, z * 128 : z * 128 + 128] = result[:half]
            blocks[8 + n, :, z * 128 : z * 128 + 128] = result[half:]
    for n in range(PARTS, DEEP):
        blocks[n] = jnp.zeros_like(blocks[n])
    for offset, ref in enumerate((keep_ref, right_ref, left_ref)):
        first = (part + offset) % 3
        for m in range(6):
            ref[m] = blocks[first + 3 * m]


def down_kernel(place_ref, own_ref, before_ref, behind_ref, edge_ref, down_ref, near_own_ref, near_ref, far_ref, hidden):
    part = place_ref[1]
    half = near_own_ref.shape[0]
    before = jnp.where(part == 0, 2, (part + 2) % 3)
    behind = jnp.where(part == PARTS - 1, 1, (part + 1) % 3)
    first_edge, last_edge = part == 0, part == PARTS - 1
    for kind in range(3):
        first = (part % 3, before, behind)[kind]
        for m in range(6):
            owner = first + 3 * m
            if kind == 0:
                value = own_ref[m]
            elif kind == 1:
                value = jnp.where(first_edge, edge_ref[m], before_ref[m])
            else:
                value = jnp.where(last_edge, edge_ref[m], behind_ref[m])
            column = pl.multiple_of(owner % 8 * 128, 128)
            for chunk in range(2):
                row = pl.multiple_of((owner // 8 * 2 + chunk) * half, 16)
                hidden[pl.ds(row, half), pl.ds(column, 128)] = value[chunk * half : (chunk + 1) * half]
    out = lax.dot_general(hidden[: 4 * half], down_ref[...], (((1,), (1,)), ((), ())),
                          preferred_element_type=jnp.float32).astype(jnp.bfloat16)
    near_own_ref[...] = out[:half]
    far_ref[0] = out[half : 2 * half]
    near_ref[...] = out[2 * half : 3 * half]
    far_ref[1] = out[3 * half :]


def combine_kernel(up_ref, down_ref, mask_ref, share_ref, *refs):
    back_refs, out_up_ref, out_down_ref = refs[:GROUPS], refs[GROUPS], refs[GROUPS + 1]
    tokens = up_ref.shape[1]
    total = jnp.concatenate([up_ref[...], down_ref[...]], axis=1).astype(jnp.float32)
    for k in range(GROUPS):
        placed = lax.dot_general(back_refs[k][...], mask_ref[k], (((0,), (0,)), ((), ())),
                                 preferred_element_type=jnp.float32)
        total = total + share_ref[k : k + 1] * placed
    out_up_ref[...] = total[:, :tokens].astype(jnp.bfloat16)
    out_down_ref[...] = total[:, tokens:].astype(jnp.bfloat16)


RIGHT = [(i, i + 1) for i in range(PARTS - 1)]
LEFT = [(i + 1, i) for i in range(PARTS - 1)]
RIGHT3 = [(i, i + 3) for i in range(PARTS - 3)]
LEFT3 = [(i + 3, i) for i in range(PARTS - 3)]
EDGE = [(0, 2), (PARTS - 1, PARTS - 3)]
EDGE3 = [(0, 6), (1, 7), (2, 8), (15, 9)]
EDGE3_MORE = [(13, 7), (14, 8)]
SWAP9 = [(i, i + 9) for i in range(7)] + [(i + 9, i) for i in range(7)]


def back(pairs):
    return [(b, a) for a, b in pairs]


def sum_chunk(place, first, second, gate_w, up_w, after=()):
    part = place[1]
    half, width = first.shape
    shapes = (jax.ShapeDtypeStruct((6, half, 256), jnp.float32),) * 3
    keep, right, left = call(up_kernel, shapes, [SMEM] + [VMEM] * 4, (place, first, second, gate_w, up_w),
                             scratch=[pltpu.VMEM((DEEP, half, 256), jnp.float32)], after=after,
                             flops=2 * 2 * half * width * 2048, moved=4 * width * 1024)
    right, left = right.astype(SUM), left.astype(SUM)
    got = [along(right, RIGHT), along(left, LEFT), along(jnp.where(part == 0, left, right), EDGE)]
    for value in got:
        keep = keep + value.astype(jnp.float32)
    return keep


def sum_pairs(place, keep):
    part = place[1]
    keep = keep.reshape((2, 3) + keep.shape[1:])

    def of_class(offset):
        return lax.dynamic_index_in_dim(keep, (part // 3 + offset) % 3, 1, keepdims=False)

    right, left = of_class(1).astype(SUM), of_class(2).astype(SUM)
    got = [along(right, RIGHT3), along(left, LEFT3), along(jnp.where(part < 3, left, right), EDGE3),
           along(right, EDGE3_MORE)]
    total = of_class(0)
    for value in got:
        total = total + value.astype(jnp.float32)
    return total


def hidden_blocks(place, total):
    part = place[1]
    upper = part >= 9
    sent = jnp.where(upper, total[0], total[1]).astype(SUM)
    value = jnp.where(upper, total[1], total[0]) + along(sent, SWAP9).astype(jnp.float32)
    own = (jax.nn.silu(value[:, :128]) * value[:, 128:]).astype(jnp.bfloat16)
    other = along(own, SWAP9)
    pair = jnp.stack([jnp.where(upper, other, own), jnp.where(upper, own, other)])
    place3 = part // 3
    before, behind = along(pair, RIGHT3), along(pair, LEFT3)
    edge, edge_more = along(pair, back(EDGE3)), along(pair, back(EDGE3_MORE))
    before = jnp.where(part < 3, edge, before)
    behind = jnp.where(part == 15, edge, jnp.where(part > 12, edge_more, behind))
    cases = []
    for m in range(3):
        offset = (m - place3) % 3
        cases.append(jnp.where(offset == 0, pair, jnp.where(offset == 1, behind, before)))
    third = jnp.stack(cases, axis=1).reshape((6,) + own.shape)
    return third, along(third, RIGHT), along(third, LEFT), along(third, back(EDGE))


def local(held_up, held_down, routes_up, routes_down, gates_up, gates_down, capacity, w_gate, w_up, w_down):
    index = lax.axis_index("expert")
    place = jnp.stack([index // PARTS, index % PARTS]).astype(jnp.int32)
    up_rows, down_rows = held_up[0].T, held_down[0].T
    width, tokens = up_rows.shape
    cap = 8 * max(1, tokens * 5 // 64)
    slot = jax.ShapeDtypeStruct((cap, width), jnp.bfloat16)
    two = jax.ShapeDtypeStruct((2, cap, width), jnp.bfloat16)
    one = jax.ShapeDtypeStruct((1, cap, width), jnp.bfloat16)
    shapes = (slot, two, one, jax.ShapeDtypeStruct((GROUPS, cap, 2 * tokens), jnp.bfloat16),
              jax.ShapeDtypeStruct((8, 2 * tokens), jnp.float32))
    own, sent, across, mask, share = call(
        functools.partial(route_kernel, cap), shapes, [SMEM] + [VMEM] * 6 + [SMEM],
        (place, up_rows, down_rows, routes_up[0].T, routes_down[0].T, gates_up[0].T, gates_down[0].T, capacity),
        flops=2 * 4 * cap * 256 * width, moved=10**6)
    got = swap(sent, 32)
    far = swap(jnp.concatenate([across, got[1:]]), 16)
    near_sums = sum_chunk(place, own, got[0], w_gate[0], w_up[0])
    far_sums = sum_chunk(place, far[0], far[1], w_gate[0], w_up[0], after=(near_sums,))
    sums = sum_pairs(place, jnp.concatenate([near_sums, far_sums], axis=1))
    third = hidden_blocks(place, sums)
    near_own, near, far = call(down_kernel, (slot, slot, two), [SMEM] + [VMEM] * 5, (place, *third, w_down[0]),
                               scratch=[pltpu.VMEM((6 * cap, 1024), jnp.bfloat16)],
                               flops=2 * 4 * cap * width * 1024, moved=2 * width * 1024)
    far = swap(far, 16)
    near = swap(jnp.stack([near, far[1]]), 32)
    back_slots = (near_own, far[0], near[0], near[1])
    rows = jax.ShapeDtypeStruct((width, tokens), jnp.bfloat16)
    out_up, out_down = call(combine_kernel, (rows, rows), [VMEM] * (4 + GROUPS),
                            (up_rows, down_rows, mask, share, *back_slots),
                            flops=2 * 4 * cap * 256 * width, moved=10**6)
    return shift(out_up, "section", 1).T[None], shift(out_down, "section", -1).T[None]


def solution(mesh):
    rows = P("section", None, "expert")
    table = P("section", None, None)
    weight = P("section", "expert", None)
    return jax.shard_map(
        local,
        mesh=mesh,
        in_specs=(rows, rows, table, table, table, table, P("section", None), weight, weight, weight),
        out_specs=(rows, rows),
        check_vma=False,
    )
```

```python
import functools

import jax
import jax.numpy as jnp
from jax import lax
from jax.experimental import pallas as pl
from jax.experimental.pallas import tpu as pltpu
from jax.sharding import PartitionSpec as P

SUM = jnp.float16
PARTS = 16
GROUPS = 4
VMEM = pltpu.VMEM
SMEM = pltpu.SMEM
VMEM_LIMIT = 40 * 1024 * 1024


NEAR = 4


def quads():
    count = lax.axis_size("expert")
    return [list(range(first, first + NEAR)) for first in range(0, count, NEAR)]


def swap(value, pattern):
    count = lax.axis_size("expert")
    return lax.ppermute(value, "expert", [(i, i ^ pattern) for i in range(count)])


def shift(value, axis, steps):
    count = lax.axis_size(axis)
    return lax.ppermute(value, axis, [(i, (i + steps) % count) for i in range(count)])


def call(kernel, out_shape, in_spaces, args, scratch=(), after=(), vmem=VMEM_LIMIT, flops=0, moved=0):
    taken = len(args)

    def body(*refs):
        kernel(*refs[:taken], *refs[taken + len(after) :])

    return pl.pallas_call(
        body,
        out_shape=out_shape,
        in_specs=[pl.BlockSpec(memory_space=space) for space in in_spaces + [pl.ANY] * len(after)],
        out_specs=jax.tree.map(lambda _: pl.BlockSpec(memory_space=VMEM), out_shape),
        scratch_shapes=list(scratch),
        compiler_params=pltpu.CompilerParams(vmem_limit_bytes=vmem),
        cost_estimate=pl.CostEstimate(flops=flops, bytes_accessed=moved, transcendentals=0),
    )(*args, *after)


def pack(first, second, ref):
    for n in range(3):
        ref[n] = first[:, n * 128 : n * 128 + 128]
        ref[3 + n] = second[:, n * 128 : n * 128 + 128]
    ref[6] = jnp.concatenate([first[:, 384:], second[:, 384:]], axis=1)


def unpack(ref):
    last = ref[6]
    return (jnp.concatenate([ref[0], ref[1], ref[2], last[:, :64]], axis=1),
            jnp.concatenate([ref[3], ref[4], ref[5], last[:, 64:]], axis=1))


def route_kernel(cap, place_ref, up_ref, down_ref, ru_ref, rd_ref, gu_ref, gd_ref, capacity_ref,
                 own_ref, sent_ref, across_ref, mask_ref, share_ref, slots):
    group = place_ref[0]
    tokens = up_ref.shape[1]
    rows = 2 * tokens
    start = pl.multiple_of(group * tokens, tokens)
    routes = jnp.concatenate([ru_ref[:, pl.ds(start, tokens)], rd_ref[:, pl.ds(start, tokens)]], axis=1)
    gates = jnp.concatenate([gu_ref[:, pl.ds(start, tokens)], gd_ref[:, pl.ds(start, tokens)]], axis=1)
    hits, shares = [], []
    for e in range(GROUPS):
        match = routes == e
        hits.append(jnp.sum(jnp.where(match, 1.0, 0.0), axis=0, keepdims=True))
        shares.append(jnp.sum(jnp.where(match, gates, 0.0), axis=0, keepdims=True))
    pad = [jnp.zeros((8 - GROUPS, rows), jnp.float32)]
    hit = jnp.concatenate(hits + pad, axis=0)
    share_ref[...] = jnp.concatenate(shares + pad, axis=0)
    before = lax.broadcasted_iota(jnp.int32, (rows, rows), 0) < lax.broadcasted_iota(jnp.int32, (rows, rows), 1)
    rank = jnp.dot(hit.astype(jnp.bfloat16), jnp.where(before, 1.0, 0.0).astype(jnp.bfloat16),
                   preferred_element_type=jnp.float32)
    block = jnp.concatenate([up_ref[...], down_ref[...]], axis=1)
    slot_ids = lax.broadcasted_iota(jnp.int32, (cap, rows), 0)
    for e in range(GROUPS):
        limit = capacity_ref[0, e].astype(jnp.float32)
        kept = (hit[e : e + 1] > 0.5) & (rank[e : e + 1] < limit)
        target = jnp.where(kept, rank[e : e + 1], -1.0).astype(jnp.int32)
        mask = jnp.where(target == slot_ids, 1.0, 0.0).astype(jnp.bfloat16)
        mask_ref[e] = mask
        slots[group ^ e] = lax.dot_general(
            mask, block, (((1,), (1,)), ((), ())), preferred_element_type=jnp.float32
        ).astype(jnp.bfloat16)
    own_ref[...] = slots[0]
    pack(slots[1], jnp.zeros_like(slots[1]), across_ref)
    pack(slots[2], slots[3], sent_ref)


def up_kernel(far, place_ref, *refs):
    part = place_ref[1]
    if far:
        packed_ref, gate_ref, up_ref, out_ref = refs
        first, second = unpack(packed_ref)
    else:
        own_ref, packed_ref, across_ref, gate_ref, up_ref, out_ref, message_ref = refs
        first, second = own_ref[...], unpack(packed_ref)[0]
        message_ref[:3] = across_ref[:3]
        message_ref[3:6] = packed_ref[3:6]
        message_ref[6] = jnp.concatenate([across_ref[6][:, :64], packed_ref[6][:, 64:]], axis=1)
    half = first.shape[0]
    x = jnp.concatenate([first, second], axis=0)
    upper = part // 8 == 1
    for q in range(NEAR):
        for differs in range(2):
            start = pl.multiple_of(((differs ^ (part // 4 % 2)) * NEAR + q) * 128, 128)
            for z, ref in enumerate((gate_ref, up_ref)):
                result = jnp.dot(x, ref[:, pl.ds(start, 128)], preferred_element_type=jnp.float32)
                one, two = result[:half], result[half:]
                out_ref[q, differs * 2, :, z * 128 : z * 128 + 128] = jnp.where(upper, two, one)
                out_ref[q, differs * 2 + 1, :, z * 128 : z * 128 + 128] = jnp.where(upper, one, two)


def hidden_kernel(sums_ref, out_ref):
    value = sums_ref[...]
    out_ref[...] = (jax.nn.silu(value[:, :128]) * value[:, 128:]).astype(jnp.bfloat16)


def down_kernel(place_ref, blocks_ref, down_ref, own_ref, beside_ref, packed_ref, hidden):
    part = place_ref[1]
    cap = own_ref.shape[0]
    for q in range(NEAR):
        for n in range(NEAR):
            row = pl.multiple_of(((n % 2) ^ (part // 8)) * 2 * cap, 16)
            column = pl.multiple_of((((n // 2) ^ (part // 4 % 2)) * NEAR + q) * 128, 128)
            hidden[pl.ds(row, 2 * cap), pl.ds(column, 128)] = blocks_ref[q, n]
    out = lax.dot_general(hidden[...], down_ref[...], (((1,), (1,)), ((), ())),
                          preferred_element_type=jnp.float32).astype(jnp.bfloat16)
    pack(out[cap : 2 * cap], out[3 * cap :], packed_ref)
    own_ref[...] = out[:cap]
    beside = out[2 * cap : 3 * cap]
    for n in range(3):
        beside_ref[n] = beside[:, n * 128 : n * 128 + 128]
    beside_ref[3] = jnp.concatenate([beside[:, 384:]] * 2, axis=1)


def combine_kernel(place_ref, up_ref, down_ref, mask_ref, share_ref, own_ref, beside_ref, packed_ref,
                   out_up_ref, out_down_ref):
    group = place_ref[0]
    tokens = up_ref.shape[1]
    total = jnp.concatenate([up_ref[...], down_ref[...]], axis=1).astype(jnp.float32)
    near_last, far_last = beside_ref[3], beside_ref[7]
    beside = jnp.concatenate([beside_ref[0], beside_ref[1], beside_ref[2], near_last[:, :64]], axis=1)
    far = jnp.concatenate([beside_ref[4], beside_ref[5], beside_ref[6], far_last[:, 64:]], axis=1)
    for k, rows in enumerate((own_ref[...], unpack(packed_ref)[0], beside, far)):
        placed = lax.dot_general(rows, mask_ref[group ^ k], (((0,), (0,)), ((), ())),
                                 preferred_element_type=jnp.float32)
        total = total + share_ref[pl.ds(group ^ k, 1), :] * placed
    out_up_ref[...] = total[:, :tokens].astype(jnp.bfloat16)
    out_down_ref[...] = total[:, tokens:].astype(jnp.bfloat16)


def halve(kept, sent, pattern):
    return kept + swap(sent.astype(SUM), pattern).astype(jnp.float32)


def sum_chunk(place, chunk, gate_w, up_w, far, after=()):
    cap = chunk[-1].shape[1]
    shape = jax.ShapeDtypeStruct((NEAR, PARTS // NEAR, cap, 256), jnp.float32)
    shapes = (shape,) if far else (shape, jax.ShapeDtypeStruct(chunk[-1].shape, chunk[-1].dtype))
    sums, *message = call(functools.partial(up_kernel, far), shapes, [SMEM] + [VMEM] * (2 + len(chunk)),
                (place, *chunk, gate_w, up_w), after=after, vmem=VMEM_LIMIT if far else 62 * 1024 * 1024,
                flops=2 * 2 * cap * 448 * 2048, moved=2 * 10**6)
    got = lax.all_to_all(sums.astype(SUM), "expert", 0, 0, axis_index_groups=quads(), tiled=True)
    return (jnp.sum(got.astype(jnp.float32), axis=0), *message)


def local(held_up, held_down, routes_up, routes_down, gates_up, gates_down, capacity, w_gate, w_up, w_down):
    index = lax.axis_index("expert")
    place = jnp.stack([index // PARTS, index % PARTS]).astype(jnp.int32)
    up_rows, down_rows = held_up[0].T, held_down[0].T
    width, tokens = up_rows.shape
    cap = 8 * max(1, tokens * 5 // 64)
    slot = jax.ShapeDtypeStruct((cap, width), jnp.bfloat16)
    packed = jax.ShapeDtypeStruct((7, cap, 128), jnp.bfloat16)
    shapes = (slot, packed, packed, jax.ShapeDtypeStruct((GROUPS, cap, 2 * tokens), jnp.bfloat16),
              jax.ShapeDtypeStruct((8, 2 * tokens), jnp.float32))
    own, sent, across, mask, share = call(
        functools.partial(route_kernel, cap), shapes, [SMEM] + [VMEM] * 6 + [SMEM],
        (place, up_rows, down_rows, routes_up[0].T, routes_down[0].T, gates_up[0].T, gates_down[0].T, capacity),
        scratch=[pltpu.VMEM((GROUPS, cap, width), jnp.bfloat16)], vmem=62 * 1024 * 1024,
        flops=2 * 4 * cap * 256 * width, moved=10**6)
    got = swap(sent, 32)
    near_sums, message = sum_chunk(place, (own, got, across), w_gate[0], w_up[0], False)
    far_sums = sum_chunk(place, (swap(message, 16),), w_gate[0], w_up[0], True, after=(near_sums,))[0]
    sums = jnp.concatenate([near_sums, far_sums], axis=1)
    sums = halve(sums[:2], sums[2:], 4)
    sums = halve(sums[0], sums[1], 8)
    block = jax.ShapeDtypeStruct((2 * cap, 128), jnp.bfloat16)
    blocks = call(hidden_kernel, (block,), [VMEM], (sums,))[0][None]
    for pattern in (8, 4):
        blocks = jnp.concatenate([blocks, swap(blocks, pattern)])
    blocks = lax.all_gather(blocks, "expert", axis_index_groups=quads())
    near_own, near_out, far_out = call(
        down_kernel, (slot, jax.ShapeDtypeStruct((4, cap, 128), jnp.bfloat16), packed), [SMEM] + [VMEM] * 2, (place, blocks, w_down[0]),
        scratch=[pltpu.VMEM((4 * cap, 1024), jnp.bfloat16)], flops=2 * 4 * cap * width * 1024, moved=2 * width * 1024)
    returned = swap(far_out, 16)
    beside = swap(jnp.concatenate([near_out, returned[3:]]), 32)
    rows = jax.ShapeDtypeStruct((width, tokens), jnp.bfloat16)
    out_up, out_down = call(combine_kernel, (rows, rows), [SMEM] + [VMEM] * 7,
                            (place, up_rows, down_rows, mask, share, near_own, beside, returned),
                            flops=2 * 4 * cap * 256 * width, moved=10**6)
    return shift(out_up, "section", 1).T[None], shift(out_down, "section", -1).T[None]


def solution(mesh):
    rows = P("section", None, "expert")
    table = P("section", None, None)
    weight = P("section", "expert", None)
    return jax.shard_map(
        local,
        mesh=mesh,
        in_specs=(rows, rows, table, table, table, table, P("section", None), weight, weight, weight),
        out_specs=(rows, rows),
        check_vma=False,
    )
```

```python
import functools

import jax
import jax.numpy as jnp
from jax import lax
from jax.experimental import pallas as pl
from jax.experimental.pallas import tpu as pltpu
from jax.sharding import PartitionSpec as P

SUM = jnp.float16
PARTS = 16
GROUPS = 4
VMEM = pltpu.VMEM
SMEM = pltpu.SMEM
VMEM_LIMIT = 40 * 1024 * 1024


NEAR = 4


def quads():
    count = lax.axis_size("expert")
    return [list(range(first, first + NEAR)) for first in range(0, count, NEAR)]


def swap(value, pattern):
    count = lax.axis_size("expert")
    return lax.ppermute(value, "expert", [(i, i ^ pattern) for i in range(count)])


def shift(value, axis, steps):
    count = lax.axis_size(axis)
    return lax.ppermute(value, axis, [(i, (i + steps) % count) for i in range(count)])


def call(kernel, out_shape, in_spaces, args, scratch=(), after=(), vmem=VMEM_LIMIT, flops=0, moved=0):
    taken = len(args)

    def body(*refs):
        kernel(*refs[:taken], *refs[taken + len(after) :])

    return pl.pallas_call(
        body,
        out_shape=out_shape,
        in_specs=[pl.BlockSpec(memory_space=space) for space in in_spaces + [pl.ANY] * len(after)],
        out_specs=jax.tree.map(lambda _: pl.BlockSpec(memory_space=VMEM), out_shape),
        scratch_shapes=list(scratch),
        compiler_params=pltpu.CompilerParams(vmem_limit_bytes=vmem),
        cost_estimate=pl.CostEstimate(flops=flops, bytes_accessed=moved, transcendentals=0),
    )(*args, *after)


def pack(first, second, ref):
    for n in range(3):
        ref[n] = first[:, n * 128 : n * 128 + 128]
        ref[3 + n] = second[:, n * 128 : n * 128 + 128]
    ref[6] = jnp.concatenate([first[:, 384:], second[:, 384:]], axis=1)


def unpack(ref):
    last = ref[6]
    return (jnp.concatenate([ref[0], ref[1], ref[2], last[:, :64]], axis=1),
            jnp.concatenate([ref[3], ref[4], ref[5], last[:, 64:]], axis=1))


def route_kernel(cap, place_ref, up_ref, down_ref, ru_ref, rd_ref, gu_ref, gd_ref, capacity_ref,
                 own_ref, sent_ref, across_ref, mask_ref, share_ref, slots):
    group = place_ref[0]
    tokens = up_ref.shape[1]
    rows = 2 * tokens
    start = pl.multiple_of(group * tokens, tokens)
    routes = jnp.concatenate([ru_ref[:, pl.ds(start, tokens)], rd_ref[:, pl.ds(start, tokens)]], axis=1)
    gates = jnp.concatenate([gu_ref[:, pl.ds(start, tokens)], gd_ref[:, pl.ds(start, tokens)]], axis=1)
    hits, shares = [], []
    for e in range(GROUPS):
        match = routes == e
        hits.append(jnp.sum(jnp.where(match, 1.0, 0.0), axis=0, keepdims=True))
        shares.append(jnp.sum(jnp.where(match, gates, 0.0), axis=0, keepdims=True))
    pad = [jnp.zeros((8 - GROUPS, rows), jnp.float32)]
    hit = jnp.concatenate(hits + pad, axis=0)
    share_ref[...] = jnp.concatenate(shares + pad, axis=0)
    before = lax.broadcasted_iota(jnp.int32, (rows, rows), 0) < lax.broadcasted_iota(jnp.int32, (rows, rows), 1)
    rank = jnp.dot(hit.astype(jnp.bfloat16), jnp.where(before, 1.0, 0.0).astype(jnp.bfloat16),
                   preferred_element_type=jnp.float32)
    block = jnp.concatenate([up_ref[...], down_ref[...]], axis=1)
    slot_ids = lax.broadcasted_iota(jnp.int32, (cap, rows), 0)
    for e in range(GROUPS):
        limit = capacity_ref[0, e].astype(jnp.float32)
        kept = (hit[e : e + 1] > 0.5) & (rank[e : e + 1] < limit)
        target = jnp.where(kept, rank[e : e + 1], -1.0).astype(jnp.int32)
        mask = jnp.where(target == slot_ids, 1.0, 0.0).astype(jnp.bfloat16)
        mask_ref[e] = mask
        slots[group ^ e] = lax.dot_general(
            mask, block, (((1,), (1,)), ((), ())), preferred_element_type=jnp.float32
        ).astype(jnp.bfloat16)
    own_ref[...] = slots[0]
    pack(slots[1], jnp.zeros_like(slots[1]), across_ref)
    pack(slots[2], slots[3], sent_ref)


def up_kernel(far, place_ref, *refs):
    part = place_ref[1]
    if far:
        packed_ref, gate_ref, up_ref, out_ref = refs
        first, second = unpack(packed_ref)
    else:
        own_ref, packed_ref, across_ref, gate_ref, up_ref, out_ref, message_ref = refs
        first, second = own_ref[...], unpack(packed_ref)[0]
        message_ref[:3] = across_ref[:3]
        message_ref[3:6] = packed_ref[3:6]
        message_ref[6] = jnp.concatenate([across_ref[6][:, :64], packed_ref[6][:, 64:]], axis=1)
    half = first.shape[0]
    x = jnp.concatenate([first, second], axis=0)
    upper = part // 8 == 1
    for q in range(NEAR):
        for differs in range(2):
            start = pl.multiple_of(((differs ^ (part // 4 % 2)) * NEAR + q) * 128, 128)
            for z, ref in enumerate((gate_ref, up_ref)):
                result = jnp.dot(x, ref[:, pl.ds(start, 128)], preferred_element_type=jnp.float32)
                one, two = result[:half], result[half:]
                out_ref[q, differs * 2, :, z * 128 : z * 128 + 128] = jnp.where(upper, two, one)
                out_ref[q, differs * 2 + 1, :, z * 128 : z * 128 + 128] = jnp.where(upper, one, two)


def hidden_kernel(sums_ref, out_ref):
    value = sums_ref[...]
    out_ref[...] = (jax.nn.silu(value[:, :128]) * value[:, 128:]).astype(jnp.bfloat16)


def down_kernel(place_ref, blocks_ref, down_ref, own_ref, beside_ref, packed_ref, hidden):
    part = place_ref[1]
    cap = own_ref.shape[0]
    for q in range(NEAR):
        for n in range(NEAR):
            row = pl.multiple_of(((n % 2) ^ (part // 8)) * 2 * cap, 16)
            column = pl.multiple_of((((n // 2) ^ (part // 4 % 2)) * NEAR + q) * 128, 128)
            hidden[pl.ds(row, 2 * cap), pl.ds(column, 128)] = blocks_ref[q, n]
    out = lax.dot_general(hidden[...], down_ref[...], (((1,), (1,)), ((), ())),
                          preferred_element_type=jnp.float32).astype(jnp.bfloat16)
    pack(out[cap : 2 * cap], out[3 * cap :], packed_ref)
    own_ref[...] = out[:cap]
    beside = out[2 * cap : 3 * cap]
    for n in range(3):
        beside_ref[n] = beside[:, n * 128 : n * 128 + 128]
    beside_ref[3] = jnp.concatenate([beside[:, 384:]] * 2, axis=1)


def combine_kernel(place_ref, up_ref, down_ref, mask_ref, share_ref, own_ref, beside_ref, packed_ref,
                   out_up_ref, out_down_ref):
    group = place_ref[0]
    tokens = up_ref.shape[1]
    total = jnp.concatenate([up_ref[...], down_ref[...]], axis=1).astype(jnp.float32)
    near_last, far_last = beside_ref[3], beside_ref[7]
    beside = jnp.concatenate([beside_ref[0], beside_ref[1], beside_ref[2], near_last[:, :64]], axis=1)
    far = jnp.concatenate([beside_ref[4], beside_ref[5], beside_ref[6], far_last[:, 64:]], axis=1)
    for k, rows in enumerate((own_ref[...], unpack(packed_ref)[0], beside, far)):
        placed = lax.dot_general(rows, mask_ref[group ^ k], (((0,), (0,)), ((), ())),
                                 preferred_element_type=jnp.float32)
        total = total + share_ref[pl.ds(group ^ k, 1), :] * placed
    out_up_ref[...] = total[:, :tokens].astype(jnp.bfloat16)
    out_down_ref[...] = total[:, tokens:].astype(jnp.bfloat16)


def halve(kept, sent, pattern):
    return kept + swap(sent.astype(SUM), pattern).astype(jnp.float32)


def sum_chunk(place, chunk, gate_w, up_w, far, after=()):
    cap = chunk[-1].shape[1]
    shape = jax.ShapeDtypeStruct((NEAR, PARTS // NEAR, cap, 256), jnp.float32)
    shapes = (shape,) if far else (shape, jax.ShapeDtypeStruct(chunk[-1].shape, chunk[-1].dtype))
    sums, *message = call(functools.partial(up_kernel, far), shapes, [SMEM] + [VMEM] * (2 + len(chunk)),
                (place, *chunk, gate_w, up_w), after=after, vmem=VMEM_LIMIT if far else 62 * 1024 * 1024,
                flops=2 * 2 * cap * 448 * 2048, moved=2 * 10**6)
    got = lax.all_to_all(sums.astype(SUM), "expert", 0, 0, axis_index_groups=quads(), tiled=True)
    return (jnp.sum(got.astype(jnp.float32), axis=0), *message)


def local(held_up, held_down, routes_up, routes_down, gates_up, gates_down, capacity, w_gate, w_up, w_down):
    index = lax.axis_index("expert")
    place = jnp.stack([index // PARTS, index % PARTS]).astype(jnp.int32)
    up_rows, down_rows = held_up[0].T, held_down[0].T
    width, tokens = up_rows.shape
    cap = 8 * max(1, tokens * 5 // 64)
    slot = jax.ShapeDtypeStruct((cap, width), jnp.bfloat16)
    packed = jax.ShapeDtypeStruct((7, cap, 128), jnp.bfloat16)
    shapes = (slot, packed, packed, jax.ShapeDtypeStruct((GROUPS, cap, 2 * tokens), jnp.bfloat16),
              jax.ShapeDtypeStruct((8, 2 * tokens), jnp.float32))
    own, sent, across, mask, share = call(
        functools.partial(route_kernel, cap), shapes, [SMEM] + [VMEM] * 6 + [SMEM],
        (place, up_rows, down_rows, routes_up[0].T, routes_down[0].T, gates_up[0].T, gates_down[0].T, capacity),
        scratch=[pltpu.VMEM((GROUPS, cap, width), jnp.bfloat16)], vmem=62 * 1024 * 1024,
        flops=2 * 4 * cap * 256 * width, moved=10**6)
    got = swap(sent, 32)
    near_sums, message = sum_chunk(place, (own, got, across), w_gate[0], w_up[0], False)
    far_sums = sum_chunk(place, (swap(message, 16),), w_gate[0], w_up[0], True, after=(near_sums,))[0]
    sums = [halve(value[:2], value[2:], 4) for value in (near_sums, far_sums)]
    sums = jnp.concatenate([halve(value[0], value[1], 8) for value in sums])
    block = jax.ShapeDtypeStruct((2 * cap, 128), jnp.bfloat16)
    blocks = call(hidden_kernel, (block,), [VMEM], (sums,))[0][None]
    for pattern in (8, 4):
        blocks = jnp.concatenate([blocks, swap(blocks, pattern)])
    blocks = lax.all_gather(blocks, "expert", axis_index_groups=quads())
    near_own, near_out, far_out = call(
        down_kernel, (slot, jax.ShapeDtypeStruct((4, cap, 128), jnp.bfloat16), packed), [SMEM] + [VMEM] * 2, (place, blocks, w_down[0]),
        scratch=[pltpu.VMEM((4 * cap, 1024), jnp.bfloat16)], flops=2 * 4 * cap * width * 1024, moved=2 * width * 1024)
    returned = swap(far_out, 16)
    beside = swap(jnp.concatenate([near_out, returned[3:]]), 32)
    rows = jax.ShapeDtypeStruct((width, tokens), jnp.bfloat16)
    out_up, out_down = call(combine_kernel, (rows, rows), [SMEM] + [VMEM] * 7,
                            (place, up_rows, down_rows, mask, share, near_own, beside, returned),
                            flops=2 * 4 * cap * 256 * width, moved=10**6)
    return shift(out_up, "section", 1).T[None], shift(out_down, "section", -1).T[None]


def solution(mesh):
    rows = P("section", None, "expert")
    table = P("section", None, None)
    weight = P("section", "expert", None)
    return jax.shard_map(
        local,
        mesh=mesh,
        in_specs=(rows, rows, table, table, table, table, P("section", None), weight, weight, weight),
        out_specs=(rows, rows),
        check_vma=False,
    )
```

```python
import functools

import jax
import jax.numpy as jnp
from jax import lax
from jax.experimental import pallas as pl
from jax.experimental.pallas import tpu as pltpu
from jax.sharding import PartitionSpec as P

SUM = jnp.float16
PARTS = 16
GROUPS = 4
VMEM = pltpu.VMEM
SMEM = pltpu.SMEM
VMEM_LIMIT = 40 * 1024 * 1024


NEAR = 4


def quads():
    count = lax.axis_size("expert")
    return [list(range(first, first + NEAR)) for first in range(0, count, NEAR)]


def swap(value, pattern):
    count = lax.axis_size("expert")
    return lax.ppermute(value, "expert", [(i, i ^ pattern) for i in range(count)])


def shift(value, axis, steps):
    count = lax.axis_size(axis)
    return lax.ppermute(value, axis, [(i, (i + steps) % count) for i in range(count)])


def call(kernel, out_shape, in_spaces, args, scratch=(), after=(), vmem=VMEM_LIMIT, flops=0, moved=0):
    taken = len(args)

    def body(*refs):
        kernel(*refs[:taken], *refs[taken + len(after) :])

    return pl.pallas_call(
        body,
        out_shape=out_shape,
        in_specs=[pl.BlockSpec(memory_space=space) for space in in_spaces + [pl.ANY] * len(after)],
        out_specs=jax.tree.map(lambda _: pl.BlockSpec(memory_space=VMEM), out_shape),
        scratch_shapes=list(scratch),
        compiler_params=pltpu.CompilerParams(vmem_limit_bytes=vmem),
        cost_estimate=pl.CostEstimate(flops=flops, bytes_accessed=moved, transcendentals=0),
    )(*args, *after)


def pack(first, second, ref):
    for n in range(3):
        ref[n] = first[:, n * 128 : n * 128 + 128]
        ref[3 + n] = second[:, n * 128 : n * 128 + 128]
    ref[6] = jnp.concatenate([first[:, 384:], second[:, 384:]], axis=1)


def unpack(ref):
    last = ref[6]
    return (jnp.concatenate([ref[0], ref[1], ref[2], last[:, :64]], axis=1),
            jnp.concatenate([ref[3], ref[4], ref[5], last[:, 64:]], axis=1))


def route_kernel(cap, place_ref, up_ref, down_ref, ru_ref, rd_ref, gu_ref, gd_ref, capacity_ref,
                 own_ref, sent_ref, across_ref, mask_ref, share_ref, slots):
    group = place_ref[0]
    tokens = up_ref.shape[1]
    rows = 2 * tokens
    start = pl.multiple_of(group * tokens, tokens)
    routes = jnp.concatenate([ru_ref[:, pl.ds(start, tokens)], rd_ref[:, pl.ds(start, tokens)]], axis=1)
    gates = jnp.concatenate([gu_ref[:, pl.ds(start, tokens)], gd_ref[:, pl.ds(start, tokens)]], axis=1)
    hits, shares = [], []
    for e in range(GROUPS):
        match = routes == e
        hits.append(jnp.sum(jnp.where(match, 1.0, 0.0), axis=0, keepdims=True))
        shares.append(jnp.sum(jnp.where(match, gates, 0.0), axis=0, keepdims=True))
    pad = [jnp.zeros((8 - GROUPS, rows), jnp.float32)]
    hit = jnp.concatenate(hits + pad, axis=0)
    share_ref[...] = jnp.concatenate(shares + pad, axis=0)
    before = lax.broadcasted_iota(jnp.int32, (rows, rows), 0) < lax.broadcasted_iota(jnp.int32, (rows, rows), 1)
    rank = jnp.dot(hit.astype(jnp.bfloat16), jnp.where(before, 1.0, 0.0).astype(jnp.bfloat16),
                   preferred_element_type=jnp.float32)
    block = jnp.concatenate([up_ref[...], down_ref[...]], axis=1)
    slot_ids = lax.broadcasted_iota(jnp.int32, (cap, rows), 0)
    for e in range(GROUPS):
        limit = capacity_ref[0, e].astype(jnp.float32)
        kept = (hit[e : e + 1] > 0.5) & (rank[e : e + 1] < limit)
        target = jnp.where(kept, rank[e : e + 1], -1.0).astype(jnp.int32)
        mask = jnp.where(target == slot_ids, 1.0, 0.0).astype(jnp.bfloat16)
        mask_ref[e] = mask
        slots[group ^ e] = lax.dot_general(
            mask, block, (((1,), (1,)), ((), ())), preferred_element_type=jnp.float32
        ).astype(jnp.bfloat16)
    own_ref[...] = slots[0]
    pack(slots[1], jnp.zeros_like(slots[1]), across_ref)
    pack(slots[2], slots[3], sent_ref)


def up_kernel(far, place_ref, *refs):
    part = place_ref[1]
    if far:
        packed_ref, gate_ref, up_ref, out_ref = refs
        first, second = unpack(packed_ref)
    else:
        own_ref, packed_ref, across_ref, gate_ref, up_ref, out_ref, message_ref = refs
        first, second = own_ref[...], unpack(packed_ref)[0]
        message_ref[:3] = across_ref[:3]
        message_ref[3:6] = packed_ref[3:6]
        message_ref[6] = jnp.concatenate([across_ref[6][:, :64], packed_ref[6][:, 64:]], axis=1)
    half = first.shape[0]
    x = jnp.concatenate([first, second], axis=0)
    upper = part // 8 == 1
    for q in range(NEAR):
        for differs in range(2):
            start = pl.multiple_of(((differs ^ (part // 4 % 2)) * NEAR + q) * 128, 128)
            for z, ref in enumerate((gate_ref, up_ref)):
                result = jnp.dot(x, ref[:, pl.ds(start, 128)], preferred_element_type=jnp.float32)
                one, two = result[:half], result[half:]
                out_ref[q, differs * 2, :, z * 128 : z * 128 + 128] = jnp.where(upper, two, one)
                out_ref[q, differs * 2 + 1, :, z * 128 : z * 128 + 128] = jnp.where(upper, one, two)


def hidden_kernel(sums_ref, out_ref):
    value = sums_ref[...]
    out_ref[...] = (jax.nn.silu(value[:, :128]) * value[:, 128:]).astype(jnp.bfloat16)


def down_kernel(far, place_ref, blocks_ref, down_ref, *refs):
    out_refs, hidden = refs[:-1], refs[-1]
    part = place_ref[1]
    cap = blocks_ref.shape[2]
    for q in range(NEAR):
        for n in range(NEAR):
            row = pl.multiple_of(((n % 2) ^ (part // 8)) * cap, 16)
            column = pl.multiple_of((((n // 2) ^ (part // 4 % 2)) * NEAR + q) * 128, 128)
            hidden[pl.ds(row, cap), pl.ds(column, 128)] = blocks_ref[q, n]
    out = lax.dot_general(hidden[...], down_ref[...], (((1,), (1,)), ((), ())),
                          preferred_element_type=jnp.float32).astype(jnp.bfloat16)
    if far:
        pack(out[:cap], out[cap:], out_refs[0])
        return
    out_refs[0][...] = out[:cap]
    beside = out[cap:]
    for n in range(3):
        out_refs[1][n] = beside[:, n * 128 : n * 128 + 128]
    out_refs[1][3] = jnp.concatenate([beside[:, 384:]] * 2, axis=1)


def copy_kernel(in_ref, out_ref):
    out_ref[...] = in_ref[:, : out_ref.shape[1]]


def combine_kernel(place_ref, up_ref, down_ref, mask_ref, share_ref, own_ref, beside_ref, packed_ref,
                   out_up_ref, out_down_ref):
    group = place_ref[0]
    tokens = up_ref.shape[1]
    total = jnp.concatenate([up_ref[...], down_ref[...]], axis=1).astype(jnp.float32)
    near_last, far_last = beside_ref[3], beside_ref[7]
    beside = jnp.concatenate([beside_ref[0], beside_ref[1], beside_ref[2], near_last[:, :64]], axis=1)
    far = jnp.concatenate([beside_ref[4], beside_ref[5], beside_ref[6], far_last[:, 64:]], axis=1)
    for k, rows in enumerate((own_ref[...], unpack(packed_ref)[0], beside, far)):
        placed = lax.dot_general(rows, mask_ref[group ^ k], (((0,), (0,)), ((), ())),
                                 preferred_element_type=jnp.float32)
        total = total + share_ref[pl.ds(group ^ k, 1), :] * placed
    out_up_ref[...] = total[:, :tokens].astype(jnp.bfloat16)
    out_down_ref[...] = total[:, tokens:].astype(jnp.bfloat16)


def halve(kept, sent, pattern):
    return kept + swap(sent.astype(SUM), pattern).astype(jnp.float32)


def sum_chunk(place, chunk, gate_w, up_w, far, after=()):
    cap = chunk[-1].shape[1]
    shape = jax.ShapeDtypeStruct((NEAR, PARTS // NEAR, cap, 256), jnp.float32)
    shapes = (shape,) if far else (shape, jax.ShapeDtypeStruct(chunk[-1].shape, chunk[-1].dtype))
    sums, *message = call(functools.partial(up_kernel, far), shapes, [SMEM] + [VMEM] * (2 + len(chunk)),
                (place, *chunk, gate_w, up_w), after=after, vmem=VMEM_LIMIT if far else 62 * 1024 * 1024,
                flops=2 * 2 * cap * 448 * 2048, moved=2 * 10**6)
    got = lax.all_to_all(sums.astype(SUM), "expert", 0, 0, axis_index_groups=quads(), tiled=True)
    return (jnp.sum(got.astype(jnp.float32), axis=0), *message)


def local(held_up, held_down, routes_up, routes_down, gates_up, gates_down, capacity, w_gate, w_up, w_down):
    index = lax.axis_index("expert")
    place = jnp.stack([index // PARTS, index % PARTS]).astype(jnp.int32)
    up_rows, down_rows = held_up[0].T, held_down[0].T
    width, tokens = up_rows.shape
    cap = 8 * max(1, tokens * 5 // 64)
    slot = jax.ShapeDtypeStruct((cap, width), jnp.bfloat16)
    packed = jax.ShapeDtypeStruct((7, cap, 128), jnp.bfloat16)
    shapes = (slot, packed, packed, jax.ShapeDtypeStruct((GROUPS, cap, 2 * tokens), jnp.bfloat16),
              jax.ShapeDtypeStruct((8, 2 * tokens), jnp.float32))
    own, sent, across, mask, share = call(
        functools.partial(route_kernel, cap), shapes, [SMEM] + [VMEM] * 6 + [SMEM],
        (place, up_rows, down_rows, routes_up[0].T, routes_down[0].T, gates_up[0].T, gates_down[0].T, capacity),
        scratch=[pltpu.VMEM((GROUPS, cap, width), jnp.bfloat16)], vmem=62 * 1024 * 1024,
        flops=2 * 4 * cap * 256 * width, moved=10**6)
    got = swap(sent, 32)
    near_sums, message = sum_chunk(place, (own, got, across), w_gate[0], w_up[0], False)
    far_sums = sum_chunk(place, (swap(message, 16),), w_gate[0], w_up[0], True, after=(near_sums,))[0]
    sums = [halve(value[:2], value[2:], 4) for value in (near_sums, far_sums)]
    sums = jnp.concatenate([halve(value[0], value[1], 8) for value in sums])
    block = jax.ShapeDtypeStruct((2 * cap, 128), jnp.bfloat16)
    blocks = call(hidden_kernel, (block,), [VMEM], (sums,))[0][None]
    for pattern in (8, 4):
        blocks = jnp.concatenate([blocks, swap(blocks, pattern)])
    tiles = jax.ShapeDtypeStruct((4, cap, 128), jnp.bfloat16)
    cost = dict(scratch=[pltpu.VMEM((2 * cap, 1024), jnp.bfloat16)])
    far_blocks = lax.all_gather(blocks[:, cap:], "expert", axis_index_groups=quads())
    far_out = call(functools.partial(down_kernel, True), (packed,), [SMEM] + [VMEM] * 2, (place, far_blocks, w_down[0]),
                   **cost)[0]
    returned = swap(far_out, 16)
    late = call(copy_kernel, (jax.ShapeDtypeStruct((4, cap, 128), jnp.bfloat16),), [VMEM], (blocks,), after=(far_out,))[0]
    near_blocks = lax.all_gather(late, "expert", axis_index_groups=quads())
    near_own, near_out = call(functools.partial(down_kernel, False), (slot, tiles), [SMEM] + [VMEM] * 2,
                              (place, near_blocks, w_down[0]), **cost)
    beside = swap(jnp.concatenate([near_out, returned[3:]]), 32)
    rows = jax.ShapeDtypeStruct((width, tokens), jnp.bfloat16)
    out_up, out_down = call(combine_kernel, (rows, rows), [SMEM] + [VMEM] * 7,
                            (place, up_rows, down_rows, mask, share, near_own, beside, returned),
                            flops=2 * 4 * cap * 256 * width, moved=10**6)
    return shift(out_up, "section", 1).T[None], shift(out_down, "section", -1).T[None]


def solution(mesh):
    rows = P("section", None, "expert")
    table = P("section", None, None)
    weight = P("section", "expert", None)
    return jax.shard_map(
        local,
        mesh=mesh,
        in_specs=(rows, rows, table, table, table, table, P("section", None), weight, weight, weight),
        out_specs=(rows, rows),
        check_vma=False,
    )
```

```python
import functools

import jax
import jax.numpy as jnp
from jax import lax
from jax.experimental import pallas as pl
from jax.experimental.pallas import tpu as pltpu
from jax.sharding import PartitionSpec as P

SUM = jnp.float16
PARTS = 16
GROUPS = 4
VMEM = pltpu.VMEM
SMEM = pltpu.SMEM
VMEM_LIMIT = 40 * 1024 * 1024


NEAR = 4


def quads():
    count = lax.axis_size("expert")
    return [list(range(first, first + NEAR)) for first in range(0, count, NEAR)]


def swap(value, pattern):
    count = lax.axis_size("expert")
    return lax.ppermute(value, "expert", [(i, i ^ pattern) for i in range(count)])


def shift(value, axis, steps):
    count = lax.axis_size(axis)
    return lax.ppermute(value, axis, [(i, (i + steps) % count) for i in range(count)])


def call(kernel, out_shape, in_spaces, args, scratch=(), after=(), vmem=VMEM_LIMIT, flops=0, moved=0):
    taken = len(args)

    def body(*refs):
        kernel(*refs[:taken], *refs[taken + len(after) :])

    return pl.pallas_call(
        body,
        out_shape=out_shape,
        in_specs=[pl.BlockSpec(memory_space=space) for space in in_spaces + [pl.ANY] * len(after)],
        out_specs=jax.tree.map(lambda _: pl.BlockSpec(memory_space=VMEM), out_shape),
        scratch_shapes=list(scratch),
        compiler_params=pltpu.CompilerParams(vmem_limit_bytes=vmem),
        cost_estimate=pl.CostEstimate(flops=flops, bytes_accessed=moved, transcendentals=0),
    )(*args, *after)


def pack(first, second, ref):
    for n in range(3):
        ref[n] = first[:, n * 128 : n * 128 + 128]
        ref[3 + n] = second[:, n * 128 : n * 128 + 128]
    ref[6] = jnp.concatenate([first[:, 384:], second[:, 384:]], axis=1)


def unpack(ref):
    last = ref[6]
    return (jnp.concatenate([ref[0], ref[1], ref[2], last[:, :64]], axis=1),
            jnp.concatenate([ref[3], ref[4], ref[5], last[:, 64:]], axis=1))


def route_kernel(cap, place_ref, up_ref, down_ref, ru_ref, rd_ref, gu_ref, gd_ref, capacity_ref,
                 own_ref, sent_ref, across_ref, mask_ref, share_ref, slots):
    group = place_ref[0]
    tokens = up_ref.shape[1]
    rows = 2 * tokens
    start = pl.multiple_of(group * tokens, tokens)
    routes = jnp.concatenate([ru_ref[:, pl.ds(start, tokens)], rd_ref[:, pl.ds(start, tokens)]], axis=1)
    gates = jnp.concatenate([gu_ref[:, pl.ds(start, tokens)], gd_ref[:, pl.ds(start, tokens)]], axis=1)
    hits, shares = [], []
    for e in range(GROUPS):
        match = routes == e
        hits.append(jnp.sum(jnp.where(match, 1.0, 0.0), axis=0, keepdims=True))
        shares.append(jnp.sum(jnp.where(match, gates, 0.0), axis=0, keepdims=True))
    pad = [jnp.zeros((8 - GROUPS, rows), jnp.float32)]
    hit = jnp.concatenate(hits + pad, axis=0)
    share_ref[...] = jnp.concatenate(shares + pad, axis=0)
    before = lax.broadcasted_iota(jnp.int32, (rows, rows), 0) < lax.broadcasted_iota(jnp.int32, (rows, rows), 1)
    rank = jnp.dot(hit.astype(jnp.bfloat16), jnp.where(before, 1.0, 0.0).astype(jnp.bfloat16),
                   preferred_element_type=jnp.float32)
    block = jnp.concatenate([up_ref[...], down_ref[...]], axis=1)
    slot_ids = lax.broadcasted_iota(jnp.int32, (cap, rows), 0)
    for e in range(GROUPS):
        limit = capacity_ref[0, e].astype(jnp.float32)
        kept = (hit[e : e + 1] > 0.5) & (rank[e : e + 1] < limit)
        target = jnp.where(kept, rank[e : e + 1], -1.0).astype(jnp.int32)
        mask = jnp.where(target == slot_ids, 1.0, 0.0).astype(jnp.bfloat16)
        mask_ref[e] = mask
        slots[group ^ e] = lax.dot_general(
            mask, block, (((1,), (1,)), ((), ())), preferred_element_type=jnp.float32
        ).astype(jnp.bfloat16)
    own_ref[...] = slots[0]
    pack(slots[1], jnp.zeros_like(slots[1]), across_ref)
    pack(slots[2], slots[3], sent_ref)


def up_kernel(far, place_ref, *refs):
    part = place_ref[1]
    if far:
        packed_ref, gate_ref, up_ref, out_ref = refs
        first, second = unpack(packed_ref)
    else:
        own_ref, packed_ref, across_ref, gate_ref, up_ref, out_ref, message_ref = refs
        first, second = own_ref[...], unpack(packed_ref)[0]
        message_ref[:3] = across_ref[:3]
        message_ref[3:6] = packed_ref[3:6]
        message_ref[6] = jnp.concatenate([across_ref[6][:, :64], packed_ref[6][:, 64:]], axis=1)
    half = first.shape[0]
    x = jnp.concatenate([first, second], axis=0)
    upper = part // 8 == 1
    for q in range(NEAR):
        for differs in range(2):
            start = pl.multiple_of(((differs ^ (part // 4 % 2)) * NEAR + q) * 128, 128)
            for z, ref in enumerate((gate_ref, up_ref)):
                result = jnp.dot(x, ref[:, pl.ds(start, 128)], preferred_element_type=jnp.float32)
                one, two = result[:half], result[half:]
                out_ref[q, differs * 2, :, z * 128 : z * 128 + 128] = jnp.where(upper, two, one)
                out_ref[q, differs * 2 + 1, :, z * 128 : z * 128 + 128] = jnp.where(upper, one, two)


def hidden_kernel(sums_ref, out_ref):
    value = sums_ref[...]
    out_ref[...] = (jax.nn.silu(value[:, :128]) * value[:, 128:]).astype(jnp.bfloat16)


def down_kernel(place_ref, blocks_ref, down_ref, own_ref, beside_ref, packed_ref, hidden):
    part = place_ref[1]
    cap = own_ref.shape[0]
    for q in range(NEAR):
        for n in range(NEAR):
            row = pl.multiple_of(((n % 2) ^ (part // 8)) * 2 * cap, 16)
            column = pl.multiple_of((((n // 2) ^ (part // 4 % 2)) * NEAR + q) * 128, 128)
            hidden[pl.ds(row, 2 * cap), pl.ds(column, 128)] = blocks_ref[q, n]
    out = lax.dot_general(hidden[...], down_ref[...], (((1,), (1,)), ((), ())),
                          preferred_element_type=jnp.float32).astype(jnp.bfloat16)
    pack(out[cap : 2 * cap], out[3 * cap :], packed_ref)
    own_ref[...] = out[:cap]
    beside = out[2 * cap : 3 * cap]
    for n in range(3):
        beside_ref[n] = beside[:, n * 128 : n * 128 + 128]
    beside_ref[3] = jnp.concatenate([beside[:, 384:]] * 2, axis=1)


def combine_kernel(place_ref, up_ref, down_ref, mask_ref, share_ref, own_ref, beside_ref, packed_ref,
                   out_up_ref, out_down_ref):
    group = place_ref[0]
    tokens = up_ref.shape[1]
    total = jnp.concatenate([up_ref[...], down_ref[...]], axis=1).astype(jnp.float32)
    near_last, far_last = beside_ref[3], beside_ref[7]
    beside = jnp.concatenate([beside_ref[0], beside_ref[1], beside_ref[2], near_last[:, :64]], axis=1)
    far = jnp.concatenate([beside_ref[4], beside_ref[5], beside_ref[6], far_last[:, 64:]], axis=1)
    for k, rows in enumerate((own_ref[...], unpack(packed_ref)[0], beside, far)):
        placed = lax.dot_general(rows, mask_ref[group ^ k], (((0,), (0,)), ((), ())),
                                 preferred_element_type=jnp.float32)
        total = total + share_ref[pl.ds(group ^ k, 1), :] * placed
    out_up_ref[...] = total[:, :tokens].astype(jnp.bfloat16)
    out_down_ref[...] = total[:, tokens:].astype(jnp.bfloat16)


def halve(kept, sent, pattern):
    return kept + swap(sent.astype(SUM), pattern).astype(jnp.float32)


def sum_chunk(place, chunk, gate_w, up_w, far, after=()):
    cap = chunk[-1].shape[1]
    shape = jax.ShapeDtypeStruct((NEAR, PARTS // NEAR, cap, 256), jnp.float32)
    shapes = (shape,) if far else (shape, jax.ShapeDtypeStruct(chunk[-1].shape, chunk[-1].dtype))
    sums, *message = call(functools.partial(up_kernel, far), shapes, [SMEM] + [VMEM] * (2 + len(chunk)),
                (place, *chunk, gate_w, up_w), after=after, vmem=VMEM_LIMIT if far else 62 * 1024 * 1024,
                flops=2 * 2 * cap * 448 * 2048, moved=2 * 10**6)
    got = lax.all_to_all(sums.astype(SUM), "expert", 0, 0, axis_index_groups=quads(), tiled=True)
    return (jnp.sum(got.astype(jnp.float32), axis=0), *message)


def local(held_up, held_down, routes_up, routes_down, gates_up, gates_down, capacity, w_gate, w_up, w_down):
    index = lax.axis_index("expert")
    place = jnp.stack([index // PARTS, index % PARTS]).astype(jnp.int32)
    up_rows, down_rows = held_up[0].T, held_down[0].T
    width, tokens = up_rows.shape
    cap = 8 * max(1, tokens * 5 // 64)
    slot = jax.ShapeDtypeStruct((cap, width), jnp.bfloat16)
    packed = jax.ShapeDtypeStruct((7, cap, 128), jnp.bfloat16)
    shapes = (slot, packed, packed, jax.ShapeDtypeStruct((GROUPS, cap, 2 * tokens), jnp.bfloat16),
              jax.ShapeDtypeStruct((8, 2 * tokens), jnp.float32))
    own, sent, across, mask, share = call(
        functools.partial(route_kernel, cap), shapes, [SMEM] + [VMEM] * 6 + [SMEM],
        (place, up_rows, down_rows, routes_up[0].T, routes_down[0].T, gates_up[0].T, gates_down[0].T, capacity),
        scratch=[pltpu.VMEM((GROUPS, cap, width), jnp.bfloat16)], vmem=62 * 1024 * 1024,
        flops=2 * 4 * cap * 256 * width, moved=10**6)
    got = swap(sent, 32)
    near_sums, message = sum_chunk(place, (own, got, across), w_gate[0], w_up[0], False)
    far_sums = sum_chunk(place, (swap(message, 16),), w_gate[0], w_up[0], True, after=(near_sums,))[0]
    block = jax.ShapeDtypeStruct((cap, 128), jnp.bfloat16)
    chunks = []
    for value in (near_sums, far_sums):
        value = halve(value[:2], value[2:], 4)
        value = halve(value[0], value[1], 8)
        own_block = call(hidden_kernel, (block,), [VMEM], (value,))[0][None]
        chunks.append((own_block, swap(own_block, 8)))
    blocks = jnp.concatenate([jnp.concatenate(pair, axis=1) for pair in zip(*chunks)])
    blocks = jnp.concatenate([blocks, swap(blocks, 4)])
    blocks = lax.all_gather(blocks, "expert", axis_index_groups=quads())
    near_own, near_out, far_out = call(
        down_kernel, (slot, jax.ShapeDtypeStruct((4, cap, 128), jnp.bfloat16), packed), [SMEM] + [VMEM] * 2, (place, blocks, w_down[0]),
        scratch=[pltpu.VMEM((4 * cap, 1024), jnp.bfloat16)], flops=2 * 4 * cap * width * 1024, moved=2 * width * 1024)
    returned = swap(far_out, 16)
    beside = swap(jnp.concatenate([near_out, returned[3:]]), 32)
    rows = jax.ShapeDtypeStruct((width, tokens), jnp.bfloat16)
    out_up, out_down = call(combine_kernel, (rows, rows), [SMEM] + [VMEM] * 7,
                            (place, up_rows, down_rows, mask, share, near_own, beside, returned),
                            flops=2 * 4 * cap * 256 * width, moved=10**6)
    return shift(out_up, "section", 1).T[None], shift(out_down, "section", -1).T[None]


def solution(mesh):
    rows = P("section", None, "expert")
    table = P("section", None, None)
    weight = P("section", "expert", None)
    return jax.shard_map(
        local,
        mesh=mesh,
        in_specs=(rows, rows, table, table, table, table, P("section", None), weight, weight, weight),
        out_specs=(rows, rows),
        check_vma=False,
    )
```
